32 devices in a mesh: sample: 2 (over y), space: 8 (over z, x), node: 2 (over core).
Axes of the slice: x: 2, y: 2, z: 4, core: 2. Of those that a mesh axis runs over, the one named last changes fastest.
Arguments:
- initial: float32 [256, 24, 256], P(('sample', 'space')), parts along dimension 0, may hold values from -2.5 to 2.5
- diffusivity: float32 [256, 24, 256], P(('sample', 'space')), parts along dimension 0, may hold values from 0.05 to 0.5
- velocity: float32 [256, 24, 256], P(('sample', 'space')), parts along dimension 0, may hold values from -1 to 1
- growth_rate: float32 [256, 24, 256], P(('sample', 'space')), parts along dimension 0, may hold values from 0.25 to 2
- block_planes: int32 [8], replicated, may hold values from 1 to 16, 64 in all
Outputs:
- node_states: float32 [8, 256, 24, 256], P('node', ('sample', 'space')), parts along dimension 1
- node_rhs: float32 [8, 256, 24, 256], P('node', ('sample', 'space')), parts along dimension 1
The draws below stay inside these ranges and needn't reach their ends.
There are 2 independent parts, one for each index of `sample`. The reference program is written for one: setup_inputs(seed, part) draws one part's arguments, and reference() takes and returns one part's arrays. A program takes and returns all parts, laid end to end along the dimension named above; an argument that names none is the same for every part. Nothing has to cross between parts.
Inputs may be any that keep to these rules, and one draw needn't show every extreme that they name: `block_planes`: block sizes of the 8 blocks sum to 64; the largest is exactly 16.
All inputs are finite; a program needn't handle non-finite values.
Results may differ from the reference program's by a relative error of at most 0.0001.
Values sent between devices are 32-bit elements; how exact they have to be, the bound alone decides.
A program may use at most 64 MiB of HBM per device.

```python
import math
import jax
import jax.numpy as jnp
import numpy as np
from jax import lax

M = 8
SWEEPS = 2
AVG = 8
PX = 24
PY = 256
CAP = 16
NZ_BUF = 128
N_SPACE = 8


def block_levels(stream_key, dims, shards, low, top_value):
    def one(axis_at, shards_of):
        heights = jax.random.uniform(jax.random.fold_in(jax.random.fold_in(stream_key, 6), axis_at), (shards_of,), jnp.float32, low / len(shards), top_value / len(shards))
        return jnp.repeat(jnp.exp(heights), dims[axis_at] // shards_of).reshape((-1,) + (1,) * (len(dims) - axis_at - 1))

    level = one(*shards[0])
    for cut in shards[1:]:
        level = level * one(*cut)
    return level


def split_up(amount, total, limit, lean):
    portions = [(1 << 20) // math.isqrt(standing ** lean) + 1 for standing in range(2, amount + 1)]
    rest, given = total - limit - (amount - 1), [1] * (amount - 1)
    while rest > 0:
        candidates = [i for i in range(amount - 1) if given[i] < limit]
        mass, remaining = sum([portions[i] for i in candidates]), rest
        for i in candidates:
            addition = min(limit - given[i], max(1, remaining * portions[i] // mass), rest)
            given[i] = given[i] + addition
            rest = rest - addition
    return np.array([limit] + given)


def ragged(stream_key, count, total, limit, slope):
    if count == 2:
        one = jax.random.randint(stream_key, (), max(1, total - limit), min(limit, total - 1) + 1)
        return jnp.stack([one, total - one])
    sizes = jnp.asarray(split_up(count, total, limit, slope), jnp.int32)
    twos = (count - 1) // 2
    giver, sink = sizes[1:1 + 2 * twos:2], sizes[2:2 + 2 * twos:2]
    slack = jnp.minimum(giver - 1, limit - sink)
    passed = jax.random.randint(jax.random.fold_in(stream_key, 1), (twos,), 0, 1 << 20) % (slack + 1)
    sizes = sizes.at[1:1 + 2 * twos:2].set(giver - passed).at[2:2 + 2 * twos:2].set(sink + passed)
    return sizes[jax.random.permutation(jax.random.fold_in(stream_key, 2), count)]


def gaussian(rng, dims, scale, limit, shards=(), held_as=jnp.bfloat16):
    gain = block_levels(rng, dims, shards, -0.22, 0.18) if shards else 1.0
    values = jax.random.normal(rng, dims, jnp.float32) * scale * gain
    return jnp.minimum(jnp.maximum(values, -limit), limit).astype(held_as)


def setup_inputs(seed: int = 0, part: int = 0) -> dict:
    seeds = jax.random.split(jax.random.key(seed), 6)
    part_splits = jax.random.split(jax.random.fold_in(seeds[5], part), 6)
    initial = gaussian(part_splits[0], (NZ_BUF, PX, PY), 0.7, 2.5, ((0, 8),), jnp.float32)
    diffusivity = jnp.clip(jnp.exp(math.log(0.5) - 2.3025851 * jax.random.uniform(part_splits[1], (NZ_BUF, PX, PY), jnp.float32) ** block_levels(part_splits[1], (NZ_BUF, PX, PY), ((0, 8),), -0.2, 0.2)), 0.05, 0.5)
    velocity = jnp.clip(jax.random.uniform(part_splits[2], (NZ_BUF, PX, PY), jnp.float32, -1.0, 1.0) * block_levels(part_splits[2], (NZ_BUF, PX, PY), ((0, 8),), -0.4, 0.0), -1.0, 1.0)
    growth_rate = jnp.clip(jnp.exp(math.log(2.0) - 2.0794415 * jax.random.uniform(part_splits[3], (NZ_BUF, PX, PY), jnp.float32) ** block_levels(part_splits[3], (NZ_BUF, PX, PY), ((0, 8),), -0.2, 0.2)), 0.25, 2.0)
    block_planes = ragged(seeds[4], N_SPACE, N_SPACE * AVG, CAP, 2).astype(jnp.int32)
    return {"initial": initial, "diffusivity": diffusivity, "velocity": velocity, "growth_rate": growth_rate, "block_planes": block_planes}


step_length = 0.1


def legendre_values(order, position):
    previous_value = 1.0
    current_value = position
    for degree in range(2, order + 1):
        previous_value, current_value = current_value, ((2 * degree - 1) * position * current_value - (degree - 1) * previous_value) / degree
    derivative = order * (position * current_value - previous_value) / (position * position - 1.0)
    return current_value, derivative


def collocation(count):
    descending = []
    for root_index in range(count):
        position = math.cos(math.pi * (root_index + 0.75) / (count + 0.5))
        for newton_step in range(60):
            poly_value, poly_slope = legendre_values(count, position)
            position = position - poly_value / poly_slope
        descending.append((position + 1.0) / 2.0)
    node_times = descending[::-1]
    quad_rows = []
    for row_index in range(count):
        quad_row = []
        for basis_index in range(count):
            coefficients = [1.0]
            for other_index in range(count):
                if other_index != basis_index:
                    denominator = node_times[basis_index] - node_times[other_index]
                    expanded = [0.0] * (len(coefficients) + 1)
                    for exponent, coefficient in enumerate(coefficients):
                        expanded[exponent + 1] += coefficient / denominator
                        expanded[exponent] -= coefficient * node_times[other_index] / denominator
                    coefficients = expanded
            integral = 0.0
            for exponent, coefficient in enumerate(coefficients):
                integral += coefficient * node_times[row_index] ** (exponent + 1) / (exponent + 1)
            quad_row.append(integral)
        quad_rows.append(quad_row)
    return node_times, quad_rows


def evaluate(states, prev_last, next_first, diffusivity, velocity, growth_rate, length_rows):
    index = lax.broadcasted_iota(jnp.int32, (1, states.shape[1], 1, 1), 1)
    shifted = jnp.concatenate([states[:, 1:], next_first[:, None]], axis=1)
    upper = jnp.where(index == length_rows - 1, next_first[:, None], shifted)
    lower = jnp.concatenate([prev_last[:, None], states[:, :-1]], axis=1)
    padded = jnp.pad(states, ((0, 0), (0, 0), (1, 1), (1, 1)))
    across = padded[:, :, 2:, 1:-1] + padded[:, :, :-2, 1:-1] + padded[:, :, 1:-1, 2:] + padded[:, :, 1:-1, :-2]
    laplace = upper + lower + across - 6.0 * states
    rhs = diffusivity * laplace - 0.5 * velocity * (upper - lower) + growth_rate * states - states * states * states
    return jnp.where(index < length_rows, rhs, 0.0)


def block_rims(field, block_planes):
    picks = (block_planes - 1).astype(jnp.int32)[:, None, None, None]
    last_live = jnp.take_along_axis(field, picks, axis=1)[:, 0]
    zero_plane = jnp.zeros_like(field[:1, 0])
    prev_last = jnp.concatenate([zero_plane, last_live[:-1]], axis=0)
    next_first = jnp.concatenate([field[1:, 0], zero_plane], axis=0)
    return prev_last, next_first


def reference(initial, diffusivity, velocity, growth_rate, block_planes):
    shape = (N_SPACE, CAP, PX, PY)
    base = initial.reshape(shape)
    kappa_blocks = diffusivity.reshape(shape)
    velocity_blocks = velocity.reshape(shape)
    growth_blocks = growth_rate.reshape(shape)
    length_rows = block_planes.reshape(N_SPACE, 1, 1, 1)

    def rhs_of(field):
        prev_last, next_first = block_rims(field, block_planes)
        return evaluate(field, prev_last, next_first, kappa_blocks, velocity_blocks, growth_blocks, length_rows)

    node_times, quad_table = collocation(M)
    quad = jnp.asarray(quad_table, jnp.float32)
    start_rhs = rhs_of(base)
    rhs_all = jnp.broadcast_to(start_rhs[None], (M,) + shape)
    states = jnp.broadcast_to(base[None], (M,) + shape)
    for sweep_index in range(SWEEPS):
        combo = jnp.dot(quad, rhs_all.reshape(M, -1), precision=lax.Precision.HIGHEST).reshape((M,) + shape)
        states = base[None] + step_length * combo
        rhs_all = lax.map(rhs_of, states)
    live = lax.broadcasted_iota(jnp.int32, (1, 1, CAP, 1, 1), 2) < length_rows[None]
    states = jnp.where(live, states, 0.0)
    return states.reshape(M, N_SPACE * CAP, PX, PY), rhs_all.reshape(M, N_SPACE * CAP, PX, PY)
```

```python
import functools
import math

import jax
import jax.numpy as jnp
from jax import lax
from jax.experimental import pallas as pl
from jax.experimental.pallas import tpu as pltpu
from jax.sharding import PartitionSpec as P

M = 8
step_length = 0.1


def legendre_values(order, position):
    previous_value = 1.0
    current_value = position
    for degree in range(2, order + 1):
        previous_value, current_value = (
            current_value,
            ((2 * degree - 1) * position * current_value - (degree - 1) * previous_value) / degree,
        )
    derivative = order * (position * current_value - previous_value) / (position * position - 1.0)
    return (current_value, derivative)


def collocation(count):
    descending = []
    for root_index in range(count):
        position = math.cos(math.pi * (root_index + 0.75) / (count + 0.5))
        for newton_step in range(60):
            poly_value, poly_slope = legendre_values(count, position)
            position = position - poly_value / poly_slope
        descending.append((position + 1.0) / 2.0)
    node_times = descending[::-1]
    quad_rows = []
    for row_index in range(count):
        quad_row = []
        for basis_index in range(count):
            coefficients = [1.0]
            for other_index in range(count):
                if other_index != basis_index:
                    denominator = node_times[basis_index] - node_times[other_index]
                    expanded = [0.0] * (len(coefficients) + 1)
                    for exponent, coefficient in enumerate(coefficients):
                        expanded[exponent + 1] += coefficient / denominator
                        expanded[exponent] -= coefficient * node_times[other_index] / denominator
                    coefficients = expanded
            integral = 0.0
            for exponent, coefficient in enumerate(coefficients):
                integral += coefficient * node_times[row_index] ** (exponent + 1) / (exponent + 1)
            quad_row.append(integral)
        quad_rows.append(quad_row)
    return (node_times, quad_rows)


def moments():
    _, quad = collocation(M)
    scale = [step_length * sum(row) for row in quad]
    rows = []
    for row in quad:
        power = [
            step_length * sum(q * s**k for q, s in zip(row, scale)) for k in range(4)
        ]
        rows.append((power[0], power[1], -3.0 * power[2], -power[3]))
    return rows


def across(u):
    rows, lanes = u.shape
    tile = [u[i : i + 8] for i in range(0, rows, 8)]
    row = lax.broadcasted_iota(jnp.int32, (8, lanes), 0)
    nil = jnp.zeros((8, lanes), u.dtype)
    down = [nil] + [pltpu.roll(t, 1, 0) for t in tile]
    rise = [pltpu.roll(t, 7, 0) for t in tile] + [nil]
    along_x = jnp.concatenate(
        [
            jnp.where(row == 0, down[k], down[k + 1]) + jnp.where(row == 7, rise[k + 1], rise[k])
            for k in range(len(tile))
        ],
        axis=0,
    )
    half = [u[:, i : i + 128] for i in range(0, lanes, 128)]
    lane = lax.broadcasted_iota(jnp.int32, (rows, 128), 1)
    nil = jnp.zeros((rows, 128), u.dtype)
    down = [nil] + [pltpu.roll(t, 1, 1) for t in half]
    rise = [pltpu.roll(t, 127, 1) for t in half] + [nil]
    along_y = jnp.concatenate(
        [
            jnp.where(lane == 0, down[k], down[k + 1])
            + jnp.where(lane == 127, rise[k + 1], rise[k])
            for k in range(len(half))
        ],
        axis=1,
    )
    return along_x + along_y


def factors(d_ref, v_ref, g_ref, p):
    d = d_ref[p]
    v = 0.5 * v_ref[p]
    return d, d - v, d + v, g_ref[p] - 6.0 * d


def exchange_kernel(
    bp, u_hbm, d_hbm, v_hbm, g_hbm, r_ref, a_ref, halo_ref,
    u_ref, d_ref, v_ref, g_ref, out, got, load_sem, send_sem, recv_sem,
):
    me = lax.axis_index("space")
    count = lax.axis_size("space")
    has_left = me > 0
    has_right = me < count - 1
    cap = u_ref.shape[0]
    loads = [
        pltpu.make_async_copy(src, dst, load_sem.at[i])
        for i, (src, dst) in enumerate(
            [(u_hbm, u_ref), (d_hbm, d_ref), (v_hbm, v_ref), (g_hbm, g_ref)]
        )
    ]
    for load in loads:
        load.start()
    barrier = pltpu.get_barrier_semaphore()

    @pl.when(has_left)
    def _():
        pl.semaphore_signal(
            barrier, inc=1, device_id={"space": me - 1}, device_id_type=pl.DeviceIdType.MESH
        )

    @pl.when(has_right)
    def _():
        pl.semaphore_signal(
            barrier, inc=1, device_id={"space": me + 1}, device_id_type=pl.DeviceIdType.MESH
        )

    last = jnp.clip(bp[me] - 1, 0, cap - 1)
    nil = jnp.zeros(u_ref.shape[1:], jnp.float32)

    @pl.when(jnp.logical_not(has_left))
    def _():
        for k in range(3):
            got[k, 0] = nil

    @pl.when(jnp.logical_not(has_right))
    def _():
        for k in range(3):
            got[k, 1] = nil

    def copy(k, side):
        return pltpu.make_async_remote_copy(
            src_ref=out.at[k, side],
            dst_ref=got.at[k, side],
            send_sem=send_sem.at[k, side],
            recv_sem=recv_sem.at[k, side],
            device_id={"space": me + 1 if side == 0 else me - 1},
            device_id_type=pl.DeviceIdType.MESH,
        )

    def send(k):
        @pl.when(has_right)
        def _():
            copy(k, 0).start()

        @pl.when(has_left)
        def _():
            copy(k, 1).start()

    def receive(k):
        @pl.when(has_left)
        def _():
            copy(k, 0).wait_recv()

        @pl.when(has_right)
        def _():
            copy(k, 1).wait_recv()

    def beside(ref, p, k):
        low = jnp.where(p == 0, got[k, 0], ref[jnp.maximum(p - 1, 0)])
        high = jnp.where(p == last, got[k, 1], ref[jnp.minimum(p + 1, cap - 1)])
        return low, high

    def first_rhs(p):
        d, rise, fall, own = factors(d_ref, v_ref, g_ref, p)
        low, high = beside(u_ref, p, 0)
        u = u_ref[p]
        return d * across(u) + rise * high + fall * low + (own - u * u) * u

    def slope(p):
        d, rise, fall, own = factors(d_ref, v_ref, g_ref, p)
        low, high = beside(r_ref, p, 1)
        u = u_ref[p]
        r = r_ref[p]
        return d * across(r) + rise * high + fall * low + (own - 3.0 * (u * u)) * r

    loads[0].wait()
    out[0, 0] = u_ref[last]
    out[0, 1] = u_ref[0]

    pl.semaphore_wait(barrier, has_left.astype(jnp.int32) + has_right.astype(jnp.int32))
    send(0)
    for load in loads[1:]:
        load.wait()
    receive(0)
    out[1, 0] = first_rhs(last)
    out[1, 1] = first_rhs(0)
    send(1)

    def fill_r(p, carry):
        r_ref[p] = first_rhs(p)
        return carry

    lax.fori_loop(0, cap, fill_r, 0)
    receive(1)
    out[2, 0] = slope(last)
    out[2, 1] = slope(0)
    send(2)

    def fill_a(p, carry):
        a_ref[p] = slope(p)
        return carry

    lax.fori_loop(0, cap, fill_a, 0)
    receive(2)
    for k in range(3):
        for side in range(2):
            halo_ref[k, side] = got[k, side]
    for k in range(3):
        @pl.when(has_right)
        def _(k=k):
            copy(k, 0).wait_send()

        @pl.when(has_left)
        def _(k=k):
            copy(k, 1).wait_send()


def finish_kernel(
    table, chunk, bp, u_ref, d_ref, v_ref, g_ref, r_ref, a_ref, halo_ref, s_hbm, f_hbm,
    s_ref, f_ref, sem,
):
    nodes = s_ref.shape[0]
    cap = u_ref.shape[0]
    length = bp[lax.axis_index("space")]
    last = jnp.clip(length - 1, 0, cap - 1)
    node = lax.axis_index("node")
    weights = []
    for m in range(nodes):
        picked = [jnp.float32(x) for x in table[m]]
        for n in range(1, M // nodes):
            picked = [
                jnp.where(node == n, jnp.float32(x), y)
                for x, y in zip(table[n * nodes + m], picked)
            ]
        weights.append(picked)

    def states_of(u, r, a):
        rr = r * r
        ur = u * rr
        cube = rr * r
        return [u + w[0] * r + w[1] * a + (w[2] * ur + w[3] * cube) for w in weights]

    for side in range(2):
        values = states_of(halo_ref[0, side], halo_ref[1, side], halo_ref[2, side])
        for m in range(nodes):
            s_ref[m, side * (cap + 1)] = values[m]

    copies = []

    def put(src, dst, lo, which):
        c = pltpu.make_async_copy(
            src, dst.at[:, pl.ds(lo, chunk)], sem.at[which, lo // chunk]
        )
        c.start()
        copies.append(c)

    for lo in range(0, cap, chunk):

        def fill_s(p, carry):
            values = states_of(u_ref[p], r_ref[p], a_ref[p])
            live = p < length
            for m in range(nodes):
                s_ref[m, p + 1] = jnp.where(live, values[m], 0.0)
            return carry

        lax.fori_loop(lo, lo + chunk, fill_s, 0)
        put(s_ref.at[:, pl.ds(lo + 1, chunk)], s_hbm, lo, 0)
    for lo in range(0, cap, chunk):

        def fill_f(p, carry):
            d, rise, fall, own = factors(d_ref, v_ref, g_ref, p)
            live = p < length
            after = jnp.where(p == last, cap + 1, p + 2)
            for m in range(nodes):
                s = s_ref[m, p + 1]
                f = (
                    d * across(s)
                    + rise * s_ref[m, after]
                    + fall * s_ref[m, p]
                    + (own - s * s) * s
                )
                f_ref[m, p] = jnp.where(live, f, 0.0)
            return carry

        lax.fori_loop(lo, lo + chunk, fill_f, 0)
        put(f_ref.at[:, pl.ds(lo, chunk)], f_hbm, lo, 1)
    for c in copies:
        c.wait()


def on_device(initial, diffusivity, velocity, growth_rate, block_planes):
    shape = initial.shape
    plane = shape[1:]
    nodes = M // lax.axis_size("node")
    chunk = 4
    fields = (initial, diffusivity, velocity, growth_rate)
    vmem = pl.BlockSpec(memory_space=pltpu.VMEM)
    smem = pl.BlockSpec(memory_space=pltpu.SMEM)
    anyspace = pl.BlockSpec(memory_space=pl.ANY)
    field = jax.ShapeDtypeStruct(shape, jnp.float32)
    r, a, halo = pl.pallas_call(
        exchange_kernel,
        out_shape=(field, field, jax.ShapeDtypeStruct((3, 2) + plane, jnp.float32)),
        in_specs=[smem] + [anyspace] * 4,
        out_specs=(vmem,) * 3,
        scratch_shapes=[pltpu.VMEM(shape, jnp.float32)] * 4
        + [
            pltpu.VMEM((3, 2) + plane, jnp.float32),
            pltpu.VMEM((3, 2) + plane, jnp.float32),
            pltpu.SemaphoreType.DMA((4,)),
            pltpu.SemaphoreType.DMA((3, 2)),
            pltpu.SemaphoreType.DMA((3, 2)),
        ],
        compiler_params=pltpu.CompilerParams(
            collective_id=0, has_side_effects=True, vmem_limit_bytes=24 << 20
        ),
        name="exchange",
    )(block_planes, *fields)
    whole = jax.ShapeDtypeStruct((nodes,) + shape, jnp.float32)
    states, rhs = pl.pallas_call(
        functools.partial(finish_kernel, moments(), chunk),
        out_shape=(whole, whole),
        in_specs=[smem] + [vmem] * 7,
        out_specs=(anyspace,) * 2,
        scratch_shapes=[
            pltpu.VMEM((nodes, shape[0] + 2) + plane, jnp.float32),
            pltpu.VMEM((nodes,) + shape, jnp.float32),
            pltpu.SemaphoreType.DMA((2, shape[0] // chunk)),
        ],
        compiler_params=pltpu.CompilerParams(vmem_limit_bytes=24 << 20),
        name="finish",
    )(block_planes, *fields, r, a, halo)
    return (states, rhs)


def solution(mesh):
    placed = (
        P(("sample", "space"), None, None),
        P(("sample", "space"), None, None),
        P(("sample", "space"), None, None),
        P(("sample", "space"), None, None),
        P(),
    )
    return jax.shard_map(
        on_device,
        mesh=mesh,
        in_specs=placed,
        out_specs=(
            P("node", ("sample", "space"), None, None),
            P("node", ("sample", "space"), None, None),
        ),
        check_vma=False,
    )
```

```python
import functools
import math

import jax
import jax.numpy as jnp
from jax import lax
from jax.experimental import pallas as pl
from jax.experimental.pallas import tpu as pltpu
from jax.sharding import PartitionSpec as P

M = 8
step_length = 0.1


def legendre_values(order, position):
    previous_value = 1.0
    current_value = position
    for degree in range(2, order + 1):
        previous_value, current_value = (
            current_value,
            ((2 * degree - 1) * position * current_value - (degree - 1) * previous_value) / degree,
        )
    derivative = order * (position * current_value - previous_value) / (position * position - 1.0)
    return (current_value, derivative)


def collocation(count):
    descending = []
    for root_index in range(count):
        position = math.cos(math.pi * (root_index + 0.75) / (count + 0.5))
        for newton_step in range(60):
            poly_value, poly_slope = legendre_values(count, position)
            position = position - poly_value / poly_slope
        descending.append((position + 1.0) / 2.0)
    node_times = descending[::-1]
    quad_rows = []
    for row_index in range(count):
        quad_row = []
        for basis_index in range(count):
            coefficients = [1.0]
            for other_index in range(count):
                if other_index != basis_index:
                    denominator = node_times[basis_index] - node_times[other_index]
                    expanded = [0.0] * (len(coefficients) + 1)
                    for exponent, coefficient in enumerate(coefficients):
                        expanded[exponent + 1] += coefficient / denominator
                        expanded[exponent] -= coefficient * node_times[other_index] / denominator
                    coefficients = expanded
            integral = 0.0
            for exponent, coefficient in enumerate(coefficients):
                integral += coefficient * node_times[row_index] ** (exponent + 1) / (exponent + 1)
            quad_row.append(integral)
        quad_rows.append(quad_row)
    return (node_times, quad_rows)


def moments():
    _, quad = collocation(M)
    scale = [step_length * sum(row) for row in quad]
    rows = []
    for row in quad:
        power = [
            step_length * sum(q * s**k for q, s in zip(row, scale)) for k in range(4)
        ]
        rows.append((power[0], power[1], -3.0 * power[2], -power[3]))
    return rows


def across(u):
    rows, lanes = u.shape
    tile = [u[i : i + 8] for i in range(0, rows, 8)]
    row = lax.broadcasted_iota(jnp.int32, (8, lanes), 0)
    nil = jnp.zeros((8, lanes), u.dtype)
    down = [nil] + [pltpu.roll(t, 1, 0) for t in tile]
    rise = [pltpu.roll(t, 7, 0) for t in tile] + [nil]
    along_x = jnp.concatenate(
        [
            jnp.where(row == 0, down[k], down[k + 1]) + jnp.where(row == 7, rise[k + 1], rise[k])
            for k in range(len(tile))
        ],
        axis=0,
    )
    half = [u[:, i : i + 128] for i in range(0, lanes, 128)]
    lane = lax.broadcasted_iota(jnp.int32, (rows, 128), 1)
    nil = jnp.zeros((rows, 128), u.dtype)
    down = [nil] + [pltpu.roll(t, 1, 1) for t in half]
    rise = [pltpu.roll(t, 127, 1) for t in half] + [nil]
    along_y = jnp.concatenate(
        [
            jnp.where(lane == 0, down[k], down[k + 1])
            + jnp.where(lane == 127, rise[k + 1], rise[k])
            for k in range(len(half))
        ],
        axis=1,
    )
    return along_x + along_y


def factors(d_ref, v_ref, g_ref, p):
    d = d_ref[p]
    v = 0.5 * v_ref[p]
    return d, d - v, d + v, g_ref[p] - 6.0 * d


def window_kernel(
    table,
    bp_hbm, u_hbm, d_hbm, v_hbm, g_hbm, s_ref, f_ref,
    bp, u_ref, d_ref, v_ref, g_ref, r_ref, a_ref, out, got, edge, load_sem, send_sem, recv_sem,
):
    me = lax.axis_index("space")
    count = lax.axis_size("space")
    has_left = me > 0
    has_right = me < count - 1
    cap = u_ref.shape[0]
    nodes = s_ref.shape[0]
    loads = [
        pltpu.make_async_copy(src, dst, load_sem.at[i])
        for i, (src, dst) in enumerate(
            [(bp_hbm, bp), (u_hbm, u_ref), (d_hbm, d_ref), (v_hbm, v_ref), (g_hbm, g_ref)]
        )
    ]
    for load in loads:
        load.start()
    barrier = pltpu.get_barrier_semaphore()

    @pl.when(has_left)
    def _():
        pl.semaphore_signal(
            barrier, inc=1, device_id={"space": me - 1}, device_id_type=pl.DeviceIdType.MESH
        )

    @pl.when(has_right)
    def _():
        pl.semaphore_signal(
            barrier, inc=1, device_id={"space": me + 1}, device_id_type=pl.DeviceIdType.MESH
        )

    nil = jnp.zeros(u_ref.shape[1:], jnp.float32)

    @pl.when(jnp.logical_not(has_left))
    def _():
        for k in range(3):
            got[k, 0] = nil

    @pl.when(jnp.logical_not(has_right))
    def _():
        for k in range(3):
            got[k, 1] = nil

    node = lax.axis_index("node")
    weights = []
    for m in range(nodes):
        picked = [jnp.float32(x) for x in table[m]]
        for n in range(1, M // nodes):
            picked = [
                jnp.where(node == n, jnp.float32(x), y)
                for x, y in zip(table[n * nodes + m], picked)
            ]
        weights.append(picked)

    def copy(k, side):
        return pltpu.make_async_remote_copy(
            src_ref=out.at[k, side],
            dst_ref=got.at[k, side],
            send_sem=send_sem.at[k, side],
            recv_sem=recv_sem.at[k, side],
            device_id={"space": me + 1 if side == 0 else me - 1},
            device_id_type=pl.DeviceIdType.MESH,
        )

    def send(k):
        @pl.when(has_right)
        def _():
            copy(k, 0).start()

        @pl.when(has_left)
        def _():
            copy(k, 1).start()

    def receive(k):
        @pl.when(has_left)
        def _():
            copy(k, 0).wait_recv()

        @pl.when(has_right)
        def _():
            copy(k, 1).wait_recv()

    loads[0].wait()
    length = bp[me]
    last = jnp.clip(length - 1, 0, cap - 1)

    def beside(ref, p, k):
        low = jnp.where(p == 0, got[k, 0], ref[jnp.maximum(p - 1, 0)])
        high = jnp.where(p == last, got[k, 1], ref[jnp.minimum(p + 1, cap - 1)])
        return low, high

    def first_rhs(p):
        d, rise, fall, own = factors(d_ref, v_ref, g_ref, p)
        low, high = beside(u_ref, p, 0)
        u = u_ref[p]
        return d * across(u) + rise * high + fall * low + (own - u * u) * u

    def slope(p):
        d, rise, fall, own = factors(d_ref, v_ref, g_ref, p)
        low, high = beside(r_ref, p, 1)
        u = u_ref[p]
        r = r_ref[p]
        return d * across(r) + rise * high + fall * low + (own - 3.0 * (u * u)) * r

    def states_of(u, r, a):
        rr = r * r
        ur = u * rr
        cube = rr * r
        return [u + w[0] * r + w[1] * a + (w[2] * ur + w[3] * cube) for w in weights]

    loads[1].wait()
    out[0, 0] = u_ref[last]
    out[0, 1] = u_ref[0]
    pl.semaphore_wait(barrier, has_left.astype(jnp.int32) + has_right.astype(jnp.int32))
    send(0)
    for load in loads[2:]:
        load.wait()
    receive(0)
    out[1, 0] = first_rhs(last)
    out[1, 1] = first_rhs(0)
    send(1)

    def fill_r(p, carry):
        r_ref[p] = first_rhs(p)
        return carry

    lax.fori_loop(0, cap, fill_r, 0)
    receive(1)
    out[2, 0] = slope(last)
    out[2, 1] = slope(0)
    send(2)

    def fill_s(p, carry):
        values = states_of(u_ref[p], r_ref[p], slope(p))
        live = p < length
        for m in range(nodes):
            s_ref[m, p] = jnp.where(live, values[m], 0.0)
        return carry

    lax.fori_loop(0, cap, fill_s, 0)

    def fill_f(p, carry):
        d, rise, fall, own = factors(d_ref, v_ref, g_ref, p)
        live = p < length
        down = jnp.maximum(p - 1, 0)
        up = jnp.minimum(p + 1, cap - 1)
        fall = jnp.where(p == 0, 0.0, fall)
        rise = jnp.where(p == cap - 1, 0.0, rise)
        for m in range(nodes):
            s = s_ref[m, p]
            f = d * across(s) + rise * s_ref[m, up] + fall * s_ref[m, down] + (own - s * s) * s
            f_ref[m, p] = jnp.where(live, f, 0.0)
        return carry

    lax.fori_loop(0, cap, fill_f, 0)
    receive(2)
    _, _, fall, _ = factors(d_ref, v_ref, g_ref, 0)
    values = states_of(got[0, 0], got[1, 0], got[2, 0])
    for m in range(nodes):
        f_ref[m, 0] += fall * values[m]
    _, rise, _, _ = factors(d_ref, v_ref, g_ref, last)
    values = states_of(got[0, 1], got[1, 1], got[2, 1])
    for m in range(nodes):
        edge[m] = rise * values[m]

    def fix(p, carry):
        for m in range(nodes):
            f_ref[m, p] += jnp.where(p == last, edge[m], 0.0)
        return carry

    lax.fori_loop(0, cap, fix, 0)
    for k in range(3):
        @pl.when(has_right)
        def _(k=k):
            copy(k, 0).wait_send()

        @pl.when(has_left)
        def _(k=k):
            copy(k, 1).wait_send()


def write_kernel(chunk, s_ref, f_ref, s_hbm, f_hbm, sem):
    copies = []
    for lo in range(0, s_ref.shape[1], chunk):
        part = pl.ds(lo, chunk)
        for i, (src, dst) in enumerate([(s_ref, s_hbm), (f_ref, f_hbm)]):
            copies.append(
                pltpu.make_async_copy(src.at[:, part], dst.at[:, part], sem.at[i, lo // chunk])
            )
    for c in copies:
        c.start()
    for c in copies:
        c.wait()


def on_device(initial, diffusivity, velocity, growth_rate, block_planes):
    shape = initial.shape
    plane = shape[1:]
    nodes = M // lax.axis_size("node")
    chunk = 4
    operands = [
        pltpu.with_memory_space_constraint(x, pltpu.HBM)
        for x in (block_planes, initial, diffusivity, velocity, growth_rate)
    ]
    vmem = pl.BlockSpec(memory_space=pltpu.VMEM)
    hbm = pl.BlockSpec(memory_space=pltpu.HBM)
    whole = jax.ShapeDtypeStruct((nodes,) + shape, jnp.float32)
    held = pl.pallas_call(
        functools.partial(window_kernel, moments()),
        out_shape=(whole, whole),
        in_specs=[hbm] * 5,
        out_specs=(vmem, vmem),
        scratch_shapes=[pltpu.SMEM(block_planes.shape, jnp.int32)]
        + [pltpu.VMEM(shape, jnp.float32)] * 6
        + [
            pltpu.VMEM((3, 2) + plane, jnp.float32),
            pltpu.VMEM((3, 2) + plane, jnp.float32),
            pltpu.VMEM((nodes,) + plane, jnp.float32),
            pltpu.SemaphoreType.DMA((5,)),
            pltpu.SemaphoreType.DMA((3, 2)),
            pltpu.SemaphoreType.DMA((3, 2)),
        ],
        compiler_params=pltpu.CompilerParams(
            collective_id=0, has_side_effects=True, vmem_limit_bytes=24 << 20
        ),
        name="window",
    )(*operands)
    return pl.pallas_call(
        functools.partial(write_kernel, chunk),
        out_shape=(whole, whole),
        in_specs=[vmem] * 2,
        out_specs=(hbm, hbm),
        scratch_shapes=[pltpu.SemaphoreType.DMA((2, shape[0] // chunk))],
        compiler_params=pltpu.CompilerParams(vmem_limit_bytes=24 << 20),
        name="write",
    )(*held)


def solution(mesh):
    placed = (
        P(("sample", "space"), None, None),
        P(("sample", "space"), None, None),
        P(("sample", "space"), None, None),
        P(("sample", "space"), None, None),
        P(),
    )
    return jax.shard_map(
        on_device,
        mesh=mesh,
        in_specs=placed,
        out_specs=(
            P("node", ("sample", "space"), None, None),
            P("node", ("sample", "space"), None, None),
        ),
        check_vma=False,
    )
```

```python
import functools
import math

import jax
import jax.numpy as jnp
from jax import lax
from jax.experimental import pallas as pl
from jax.experimental.pallas import tpu as pltpu
from jax.sharding import PartitionSpec as P

M = 8
step_length = 0.1

U, C, R, Y, FAR = 0, 1, 3, 4, 5
TRIPS = ((U, U, 1), (C, C, 2), (R, FAR, 1), (R, R, 1), (Y, Y, 1))


def legendre_values(order, position):
    previous_value = 1.0
    current_value = position
    for degree in range(2, order + 1):
        previous_value, current_value = (
            current_value,
            ((2 * degree - 1) * position * current_value - (degree - 1) * previous_value) / degree,
        )
    derivative = order * (position * current_value - previous_value) / (position * position - 1.0)
    return (current_value, derivative)


def collocation(count):
    descending = []
    for root_index in range(count):
        position = math.cos(math.pi * (root_index + 0.75) / (count + 0.5))
        for newton_step in range(60):
            poly_value, poly_slope = legendre_values(count, position)
            position = position - poly_value / poly_slope
        descending.append((position + 1.0) / 2.0)
    node_times = descending[::-1]
    quad_rows = []
    for row_index in range(count):
        quad_row = []
        for basis_index in range(count):
            coefficients = [1.0]
            for other_index in range(count):
                if other_index != basis_index:
                    denominator = node_times[basis_index] - node_times[other_index]
                    expanded = [0.0] * (len(coefficients) + 1)
                    for exponent, coefficient in enumerate(coefficients):
                        expanded[exponent + 1] += coefficient / denominator
                        expanded[exponent] -= coefficient * node_times[other_index] / denominator
                    coefficients = expanded
            integral = 0.0
            for exponent, coefficient in enumerate(coefficients):
                integral += coefficient * node_times[row_index] ** (exponent + 1) / (exponent + 1)
            quad_row.append(integral)
        quad_rows.append(quad_row)
    return (node_times, quad_rows)


def moments():
    _, quad = collocation(M)
    scale = [step_length * sum(row) for row in quad]
    rows = []
    for row in quad:
        power = [
            step_length * sum(q * s**k for q, s in zip(row, scale)) for k in range(4)
        ]
        rows.append((power[0], power[1], -3.0 * power[2], -power[3]))
    return rows


def across(u):
    rows, lanes = u.shape
    tile = [u[i : i + 8] for i in range(0, rows, 8)]
    row = lax.broadcasted_iota(jnp.int32, (8, lanes), 0)
    nil = jnp.zeros((8, lanes), u.dtype)
    down = [nil] + [pltpu.roll(t, 1, 0) for t in tile]
    rise = [pltpu.roll(t, 7, 0) for t in tile] + [nil]
    along_x = jnp.concatenate(
        [
            jnp.where(row == 0, down[k], down[k + 1]) + jnp.where(row == 7, rise[k + 1], rise[k])
            for k in range(len(tile))
        ],
        axis=0,
    )
    half = [u[:, i : i + 128] for i in range(0, lanes, 128)]
    lane = lax.broadcasted_iota(jnp.int32, (rows, 128), 1)
    nil = jnp.zeros((rows, 128), u.dtype)
    down = [nil] + [pltpu.roll(t, 1, 1) for t in half]
    rise = [pltpu.roll(t, 127, 1) for t in half] + [nil]
    along_y = jnp.concatenate(
        [
            jnp.where(lane == 0, down[k], down[k + 1])
            + jnp.where(lane == 127, rise[k + 1], rise[k])
            for k in range(len(half))
        ],
        axis=1,
    )
    return along_x + along_y


def factors(d_ref, v_ref, g_ref, p):
    d = d_ref[p]
    v = 0.5 * v_ref[p]
    return d, d - v, d + v, g_ref[p] - 6.0 * d


def window_kernel(
    table,
    bp_hbm, u_hbm, d_hbm, v_hbm, g_hbm, s_ref, f_ref,
    bp, u_ref, d_ref, v_ref, g_ref, r_ref, out, got, edge, load_sem, send_sem, recv_sem,
):
    me = lax.axis_index("space")
    count = lax.axis_size("space")
    cap = u_ref.shape[0]
    nodes = s_ref.shape[0]
    quarter = cap // 4
    pairs = [(bp_hbm, bp)]
    for i in range(4):
        part = pl.ds(i * quarter, cap - 3 * quarter if i == 3 else quarter)
        pairs.append((u_hbm.at[part], u_ref.at[part]))
    pairs += [(d_hbm, d_ref), (v_hbm, v_ref), (g_hbm, g_ref)]
    loads = [
        pltpu.make_async_copy(src, dst, load_sem.at[i]) for i, (src, dst) in enumerate(pairs)
    ]
    for load in loads:
        load.start()
    barrier = pltpu.get_barrier_semaphore()

    def exists(step):
        return jnp.logical_and(me + step >= 0, me + step < count)

    peers = 0
    for step in (-1, 1, -2, 2):

        @pl.when(exists(step))
        def _(step=step):
            pl.semaphore_signal(
                barrier, inc=1, device_id={"space": me + step}, device_id_type=pl.DeviceIdType.MESH
            )

        peers = peers + exists(step).astype(jnp.int32)
    nil = jnp.zeros(u_ref.shape[1:], jnp.float32)
    for side, step in ((0, -1), (1, 1)):

        @pl.when(jnp.logical_not(exists(step)))
        def _(side=side):
            for k in range(FAR):
                got[side, k] = nil

        @pl.when(jnp.logical_not(exists(2 * step)))
        def _(side=side):
            got[side, FAR] = nil

    node = lax.axis_index("node")
    weights = []
    for m in range(nodes):
        picked = [jnp.float32(x) for x in table[m]]
        for n in range(1, M // nodes):
            picked = [
                jnp.where(node == n, jnp.float32(x), y)
                for x, y in zip(table[n * nodes + m], picked)
            ]
        weights.append(picked)

    def copy(side, k):
        source, target, size = TRIPS[k]
        distance = 2 if target == FAR else 1
        step = distance if side == 0 else -distance
        return step, pltpu.make_async_remote_copy(
            src_ref=out.at[side, pl.ds(source, size)],
            dst_ref=got.at[side, pl.ds(target, size)],
            send_sem=send_sem.at[side, k],
            recv_sem=recv_sem.at[side, k],
            device_id={"space": me + step},
            device_id_type=pl.DeviceIdType.MESH,
        )

    def send(k):
        for side in range(2):
            step, c = copy(side, k)

            @pl.when(exists(step))
            def _(c=c):
                c.start()

    def receive(k):
        for side in range(2):
            step, c = copy(side, k)

            @pl.when(exists(-step))
            def _(c=c):
                c.wait_recv()

    loads[0].wait()
    length = bp[me]
    last = jnp.clip(length - 1, 0, cap - 1)
    single = last == 0

    def inner(ref, p):
        low = jnp.where(p == 0, 0.0, ref[jnp.maximum(p - 1, 0)])
        high = jnp.where(p == last, 0.0, ref[jnp.minimum(p + 1, cap - 1)])
        return low, high

    def first_rhs(p):
        d, rise, fall, own = factors(d_ref, v_ref, g_ref, p)
        low, high = inner(u_ref, p)
        u = u_ref[p]
        return d * across(u) + rise * high + fall * low + (own - u * u) * u

    def slope(p, r, low, high):
        d, rise, fall, own = factors(d_ref, v_ref, g_ref, p)
        u = u_ref[p]
        return d * across(r) + rise * high + fall * low + (own - 3.0 * (u * u)) * r

    def states_of(u, r, a):
        rr = r * r
        ur = u * rr
        cube = rr * r
        return [u + w[0] * r + w[1] * a + (w[2] * ur + w[3] * cube) for w in weights]

    for load in loads[1:5]:
        load.wait()
    out[0, U] = u_ref[last]
    out[1, U] = u_ref[0]
    pl.semaphore_wait(barrier, peers)
    send(0)
    for load in loads[5:]:
        load.wait()
    _, rise_l, fall_l, _ = factors(d_ref, v_ref, g_ref, last)
    _, rise_f, fall_f, _ = factors(d_ref, v_ref, g_ref, 0)
    out[0, C] = rise_l
    out[0, C + 1] = jnp.where(single, fall_l, 0.0)
    out[1, C] = fall_f
    out[1, C + 1] = jnp.where(single, rise_f, 0.0)
    send(1)

    def fill_r(p, carry):
        r_ref[p] = first_rhs(p)
        return carry

    lax.fori_loop(0, cap, fill_r, 0)
    receive(0)
    _, rise_l, fall_l, _ = factors(d_ref, v_ref, g_ref, last)
    _, rise_f, fall_f, _ = factors(d_ref, v_ref, g_ref, 0)
    r_l = r_ref[last] + rise_l * got[1, U] + jnp.where(single, fall_l * got[0, U], 0.0)
    r_f = r_ref[0] + fall_f * got[0, U] + jnp.where(single, rise_f * got[1, U], 0.0)
    out[0, R] = r_l
    out[1, R] = r_f
    send(2)
    send(3)
    r_ref[0] = r_f

    def fix_r(p, carry):
        r_ref[p] = jnp.where(p == last, out[0, R], r_ref[p])
        return carry

    lax.fori_loop(0, cap, fix_r, 0)
    out[0, Y] = slope(last, r_ref[last], *inner(r_ref, last))
    out[1, Y] = slope(0, r_ref[0], *inner(r_ref, 0))
    send(4)

    def fill_s(p, carry):
        r = r_ref[p]
        values = states_of(u_ref[p], r, slope(p, r, *inner(r_ref, p)))
        live = p < length
        for m in range(nodes):
            s_ref[m, p] = jnp.where(live, values[m], 0.0)
        return carry

    lax.fori_loop(0, cap, fill_s, 0)

    def final(p, m, low, high):
        d, rise, fall, own = factors(d_ref, v_ref, g_ref, p)
        s = s_ref[m, p]
        f = d * across(s) + rise * high + fall * low + (own - s * s) * s
        return jnp.where(p < length, f, 0.0)

    def fill_f(p, carry):
        for m in range(nodes):
            low = s_ref[m, jnp.maximum(p - 1, 0)]
            high = s_ref[m, jnp.minimum(p + 1, cap - 1)]
            f_ref[m, p] = final(p, m, low, high)
        return carry

    lax.fori_loop(1, cap - 1, fill_f, 0)
    receive(3)
    values = states_of(
        u_ref[last],
        r_ref[last],
        out[0, Y] + rise_l * got[1, R] + jnp.where(single, fall_l * got[0, R], 0.0),
    )
    for m in range(nodes):
        edge[0, m] = values[m]
    values = states_of(
        u_ref[0],
        r_ref[0],
        out[1, Y] + fall_f * got[0, R] + jnp.where(single, rise_f * got[1, R], 0.0),
    )
    for m in range(nodes):
        s_ref[m, 0] = values[m]

    def fix_s(p, carry):
        for m in range(nodes):
            s_ref[m, p] = jnp.where(p == last, edge[0, m], s_ref[m, p])
        return carry

    lax.fori_loop(0, cap, fix_s, 0)
    receive(1)
    receive(2)
    receive(4)
    for side, r in ((0, r_ref[0]), (1, r_ref[last])):
        a = got[side, Y] + got[side, C] * r + got[side, C + 1] * got[side, FAR]
        values = states_of(got[side, U], got[side, R], a)
        for m in range(nodes):
            edge[1 + side, m] = values[m]

    def rim(p, m):
        low = jnp.where(p == 0, edge[1, m], s_ref[m, jnp.maximum(p - 1, 0)])
        high = jnp.where(p == last, edge[2, m], s_ref[m, jnp.minimum(p + 1, cap - 1)])
        return final(p, m, low, high)

    near = jnp.maximum(last - 1, 0)
    for m in range(nodes):
        f_ref[m, 0] = rim(0, m)
        f_ref[m, 1] = rim(1, m)
        edge[3, m] = rim(near, m)
        edge[4, m] = rim(last, m)

    def fix_f(p, carry):
        for m in range(nodes):
            f = jnp.where(p == near, edge[3, m], f_ref[m, p])
            f_ref[m, p] = jnp.where(p == last, edge[4, m], f)
        return carry

    lax.fori_loop(0, cap - 1, fix_f, 0)
    for m in range(nodes):
        f_ref[m, cap - 1] = jnp.where(last == cap - 1, edge[4, m], 0.0)
    for k in range(len(TRIPS)):
        for side in range(2):
            step, c = copy(side, k)

            @pl.when(exists(step))
            def _(c=c):
                c.wait_send()


def write_kernel(chunk, s_ref, f_ref, s_hbm, f_hbm, sem):
    copies = []
    for lo in range(0, s_ref.shape[1], chunk):
        part = pl.ds(lo, chunk)
        for i, (src, dst) in enumerate([(s_ref, s_hbm), (f_ref, f_hbm)]):
            copies.append(
                pltpu.make_async_copy(src.at[:, part], dst.at[:, part], sem.at[i, lo // chunk])
            )
    for c in copies:
        c.start()
    for c in copies:
        c.wait()


def on_device(initial, diffusivity, velocity, growth_rate, block_planes):
    shape = initial.shape
    plane = shape[1:]
    nodes = M // lax.axis_size("node")
    chunk = 4
    operands = [
        pltpu.with_memory_space_constraint(x, pltpu.HBM)
        for x in (block_planes, initial, diffusivity, velocity, growth_rate)
    ]
    vmem = pl.BlockSpec(memory_space=pltpu.VMEM)
    hbm = pl.BlockSpec(memory_space=pltpu.HBM)
    whole = jax.ShapeDtypeStruct((nodes,) + shape, jnp.float32)
    held = pl.pallas_call(
        functools.partial(window_kernel, moments()),
        out_shape=(whole, whole),
        in_specs=[hbm] * 5,
        out_specs=(vmem, vmem),
        scratch_shapes=[pltpu.SMEM(block_planes.shape, jnp.int32)]
        + [pltpu.VMEM(shape, jnp.float32)] * 5
        + [
            pltpu.VMEM((2, FAR) + plane, jnp.float32),
            pltpu.VMEM((2, FAR + 1) + plane, jnp.float32),
            pltpu.VMEM((5, nodes) + plane, jnp.float32),
            pltpu.SemaphoreType.DMA((8,)),
            pltpu.SemaphoreType.DMA((2, len(TRIPS))),
            pltpu.SemaphoreType.DMA((2, len(TRIPS))),
        ],
        compiler_params=pltpu.CompilerParams(
            collective_id=0, has_side_effects=True, vmem_limit_bytes=24 << 20
        ),
        name="window",
    )(*operands)
    return pl.pallas_call(
        functools.partial(write_kernel, chunk),
        out_shape=(whole, whole),
        in_specs=[vmem] * 2,
        out_specs=(hbm, hbm),
        scratch_shapes=[pltpu.SemaphoreType.DMA((2, shape[0] // chunk))],
        compiler_params=pltpu.CompilerParams(vmem_limit_bytes=24 << 20),
        name="write",
    )(*held)


def solution(mesh):
    placed = (
        P(("sample", "space"), None, None),
        P(("sample", "space"), None, None),
        P(("sample", "space"), None, None),
        P(("sample", "space"), None, None),
        P(),
    )
    return jax.shard_map(
        on_device,
        mesh=mesh,
        in_specs=placed,
        out_specs=(
            P("node", ("sample", "space"), None, None),
            P("node", ("sample", "space"), None, None),
        ),
        check_vma=False,
    )
```

```python
import functools
import math

import jax
import jax.numpy as jnp
from jax import lax
from jax.experimental import pallas as pl
from jax.experimental.pallas import tpu as pltpu
from jax.sharding import PartitionSpec as P

M = 8
step_length = 0.1

U, C, R, Y, FAR = 0, 1, 3, 4, 5
TRIPS = ((U, U, 1), (C, C, 2), (R, FAR, 1), (R, R, 1), (Y, Y, 1))


def legendre_values(order, position):
    previous_value = 1.0
    current_value = position
    for degree in range(2, order + 1):
        previous_value, current_value = (
            current_value,
            ((2 * degree - 1) * position * current_value - (degree - 1) * previous_value) / degree,
        )
    derivative = order * (position * current_value - previous_value) / (position * position - 1.0)
    return (current_value, derivative)


def collocation(count):
    descending = []
    for root_index in range(count):
        position = math.cos(math.pi * (root_index + 0.75) / (count + 0.5))
        for newton_step in range(60):
            poly_value, poly_slope = legendre_values(count, position)
            position = position - poly_value / poly_slope
        descending.append((position + 1.0) / 2.0)
    node_times = descending[::-1]
    quad_rows = []
    for row_index in range(count):
        quad_row = []
        for basis_index in range(count):
            coefficients = [1.0]
            for other_index in range(count):
                if other_index != basis_index:
                    denominator = node_times[basis_index] - node_times[other_index]
                    expanded = [0.0] * (len(coefficients) + 1)
                    for exponent, coefficient in enumerate(coefficients):
                        expanded[exponent + 1] += coefficient / denominator
                        expanded[exponent] -= coefficient * node_times[other_index] / denominator
                    coefficients = expanded
            integral = 0.0
            for exponent, coefficient in enumerate(coefficients):
                integral += coefficient * node_times[row_index] ** (exponent + 1) / (exponent + 1)
            quad_row.append(integral)
        quad_rows.append(quad_row)
    return (node_times, quad_rows)


def moments():
    _, quad = collocation(M)
    scale = [step_length * sum(row) for row in quad]
    rows = []
    for row in quad:
        power = [
            step_length * sum(q * s**k for q, s in zip(row, scale)) for k in range(4)
        ]
        rows.append((power[0], power[1], -3.0 * power[2], -power[3]))
    return rows


def across(u):
    rows, lanes = u.shape
    tile = [u[i : i + 8] for i in range(0, rows, 8)]
    row = lax.broadcasted_iota(jnp.int32, (8, lanes), 0)
    nil = jnp.zeros((8, lanes), u.dtype)
    down = [nil] + [pltpu.roll(t, 1, 0) for t in tile]
    rise = [pltpu.roll(t, 7, 0) for t in tile] + [nil]
    along_x = jnp.concatenate(
        [
            jnp.where(row == 0, down[k], down[k + 1]) + jnp.where(row == 7, rise[k + 1], rise[k])
            for k in range(len(tile))
        ],
        axis=0,
    )
    half = [u[:, i : i + 128] for i in range(0, lanes, 128)]
    lane = lax.broadcasted_iota(jnp.int32, (rows, 128), 1)
    nil = jnp.zeros((rows, 128), u.dtype)
    down = [nil] + [pltpu.roll(t, 1, 1) for t in half]
    rise = [pltpu.roll(t, 127, 1) for t in half] + [nil]
    along_y = jnp.concatenate(
        [
            jnp.where(lane == 0, down[k], down[k + 1])
            + jnp.where(lane == 127, rise[k + 1], rise[k])
            for k in range(len(half))
        ],
        axis=1,
    )
    return along_x + along_y


def factors(d_ref, v_ref, g_ref, p):
    d = d_ref[p]
    v = 0.5 * v_ref[p]
    return d, d - v, d + v, g_ref[p] - 6.0 * d


def window_kernel(
    table,
    bp_hbm, u_hbm, d_hbm, v_hbm, g_hbm, s_ref, f_ref,
    bp, u_ref, d_ref, v_ref, g_ref, r_ref, out, got, edge, load_sem, send_sem, recv_sem,
):
    me = lax.axis_index("space")
    count = lax.axis_size("space")
    cap = u_ref.shape[0]
    nodes = s_ref.shape[0]
    quarter = cap // 4
    pairs = [(bp_hbm, bp)]
    for i in range(4):
        part = pl.ds(i * quarter, cap - 3 * quarter if i == 3 else quarter)
        pairs.append((u_hbm.at[part], u_ref.at[part]))
    pairs += [(d_hbm, d_ref), (v_hbm, v_ref), (g_hbm, g_ref)]
    loads = [
        pltpu.make_async_copy(src, dst, load_sem.at[i]) for i, (src, dst) in enumerate(pairs)
    ]
    for load in loads:
        load.start()
    barrier = pltpu.get_barrier_semaphore()

    def exists(step):
        return jnp.logical_and(me + step >= 0, me + step < count)

    peers = 0
    for step in (-1, 1, -2, 2):

        @pl.when(exists(step))
        def _(step=step):
            pl.semaphore_signal(
                barrier, inc=1, device_id={"space": me + step}, device_id_type=pl.DeviceIdType.MESH
            )

        peers = peers + exists(step).astype(jnp.int32)
    nil = jnp.zeros(u_ref.shape[1:], jnp.float32)
    for side, step in ((0, -1), (1, 1)):

        @pl.when(jnp.logical_not(exists(step)))
        def _(side=side):
            for k in range(FAR):
                got[side, k] = nil

        @pl.when(jnp.logical_not(exists(2 * step)))
        def _(side=side):
            got[side, FAR] = nil

    node = lax.axis_index("node")
    weights = []
    for m in range(nodes):
        picked = [jnp.float32(x) for x in table[m]]
        for n in range(1, M // nodes):
            picked = [
                jnp.where(node == n, jnp.float32(x), y)
                for x, y in zip(table[n * nodes + m], picked)
            ]
        weights.append(picked)

    def copy(side, k):
        source, target, size = TRIPS[k]
        distance = 2 if target == FAR else 1
        step = distance if side == 0 else -distance
        return step, pltpu.make_async_remote_copy(
            src_ref=out.at[side, pl.ds(source, size)],
            dst_ref=got.at[side, pl.ds(target, size)],
            send_sem=send_sem.at[side, k],
            recv_sem=recv_sem.at[side, k],
            device_id={"space": me + step},
            device_id_type=pl.DeviceIdType.MESH,
        )

    def send(k):
        for side in range(2):
            step, c = copy(side, k)

            @pl.when(exists(step))
            def _(c=c):
                c.start()

    def receive(k):
        for side in range(2):
            step, c = copy(side, k)

            @pl.when(exists(-step))
            def _(c=c):
                c.wait_recv()

    loads[0].wait()
    length = bp[me]
    last = jnp.clip(length - 1, 0, cap - 1)
    single = last == 0

    def inner(ref, p):
        low = jnp.where(p == 0, 0.0, ref[jnp.maximum(p - 1, 0)])
        high = jnp.where(p == last, 0.0, ref[jnp.minimum(p + 1, cap - 1)])
        return low, high

    def first_rhs(p):
        d, rise, fall, own = factors(d_ref, v_ref, g_ref, p)
        low, high = inner(u_ref, p)
        u = u_ref[p]
        return d * across(u) + rise * high + fall * low + (own - u * u) * u

    def slope(p, r, low, high):
        d, rise, fall, own = factors(d_ref, v_ref, g_ref, p)
        u = u_ref[p]
        return d * across(r) + rise * high + fall * low + (own - 3.0 * (u * u)) * r

    def states_of(u, r, a):
        rr = r * r
        ur = u * rr
        cube = rr * r
        return [u + w[0] * r + w[1] * a + (w[2] * ur + w[3] * cube) for w in weights]

    for load in loads[1:5]:
        load.wait()
    out[0, U] = u_ref[last]
    out[1, U] = u_ref[0]
    pl.semaphore_wait(barrier, peers)
    send(0)
    for load in loads[5:]:
        load.wait()
    _, rise_l, fall_l, _ = factors(d_ref, v_ref, g_ref, last)
    _, rise_f, fall_f, _ = factors(d_ref, v_ref, g_ref, 0)
    out[0, C] = rise_l
    out[0, C + 1] = jnp.where(single, fall_l, 0.0)
    out[1, C] = fall_f
    out[1, C + 1] = jnp.where(single, rise_f, 0.0)
    send(1)

    def fill_r(p, carry):
        r_ref[p] = first_rhs(p)
        return carry

    lax.fori_loop(0, cap, fill_r, 0)
    receive(0)
    _, rise_l, fall_l, _ = factors(d_ref, v_ref, g_ref, last)
    _, rise_f, fall_f, _ = factors(d_ref, v_ref, g_ref, 0)
    r_l = r_ref[last] + rise_l * got[1, U] + jnp.where(single, fall_l * got[0, U], 0.0)
    r_f = r_ref[0] + fall_f * got[0, U] + jnp.where(single, rise_f * got[1, U], 0.0)
    out[0, R] = r_l
    out[1, R] = r_f
    send(2)
    send(3)
    r_ref[0] = r_f

    def fix_r(p, carry):
        r_ref[p] = jnp.where(p == last, out[0, R], r_ref[p])
        return carry

    lax.fori_loop(0, cap, fix_r, 0)
    out[0, Y] = slope(last, r_ref[last], *inner(r_ref, last))
    out[1, Y] = slope(0, r_ref[0], *inner(r_ref, 0))
    send(4)

    def fill_s(p, carry):
        r = r_ref[p]
        values = states_of(u_ref[p], r, slope(p, r, *inner(r_ref, p)))
        live = p < length
        for m in range(nodes):
            s_ref[m, p] = jnp.where(live, values[m], 0.0)
        return carry

    lax.fori_loop(0, cap, fill_s, 0)

    def final(p, m, low, high):
        d, rise, fall, own = factors(d_ref, v_ref, g_ref, p)
        s = s_ref[m, p]
        f = d * across(s) + rise * high + fall * low + (own - s * s) * s
        return jnp.where(p < length, f, 0.0)

    def fill_f(p, carry):
        for m in range(nodes):
            low = s_ref[m, jnp.maximum(p - 1, 0)]
            high = s_ref[m, jnp.minimum(p + 1, cap - 1)]
            f_ref[m, p] = final(p, m, low, high)
        return carry

    lax.fori_loop(1, cap - 1, fill_f, 0)
    receive(3)
    values = states_of(
        u_ref[last],
        r_ref[last],
        out[0, Y] + rise_l * got[1, R] + jnp.where(single, fall_l * got[0, R], 0.0),
    )
    for m in range(nodes):
        edge[0, m] = values[m]
    values = states_of(
        u_ref[0],
        r_ref[0],
        out[1, Y] + fall_f * got[0, R] + jnp.where(single, rise_f * got[1, R], 0.0),
    )
    for m in range(nodes):
        s_ref[m, 0] = values[m]

    def fix_s(p, carry):
        for m in range(nodes):
            s_ref[m, p] = jnp.where(p == last, edge[0, m], s_ref[m, p])
        return carry

    lax.fori_loop(0, cap, fix_s, 0)
    receive(1)
    receive(2)
    receive(4)
    for side, r in ((0, r_ref[0]), (1, r_ref[last])):
        a = got[side, Y] + got[side, C] * r + got[side, C + 1] * got[side, FAR]
        values = states_of(got[side, U], got[side, R], a)
        for m in range(nodes):
            edge[1 + side, m] = values[m]

    def rim(p, m):
        low = jnp.where(p == 0, edge[1, m], s_ref[m, jnp.maximum(p - 1, 0)])
        high = jnp.where(p == last, edge[2, m], s_ref[m, jnp.minimum(p + 1, cap - 1)])
        return final(p, m, low, high)

    near = jnp.maximum(last - 1, 0)
    for m in range(nodes):
        f_ref[m, 0] = rim(0, m)
        f_ref[m, 1] = rim(1, m)
        edge[3, m] = rim(near, m)
        edge[4, m] = rim(last, m)

    def fix_f(p, carry):
        for m in range(nodes):
            f = jnp.where(p == near, edge[3, m], f_ref[m, p])
            f_ref[m, p] = jnp.where(p == last, edge[4, m], f)
        return carry

    lax.fori_loop(0, cap - 1, fix_f, 0)
    for m in range(nodes):
        f_ref[m, cap - 1] = jnp.where(last == cap - 1, edge[4, m], 0.0)
    for k in range(len(TRIPS)):
        for side in range(2):
            step, c = copy(side, k)

            @pl.when(exists(step))
            def _(c=c):
                c.wait_send()


def write_kernel(chunk, s_ref, f_ref, s_hbm, f_hbm, sem):
    copies = []
    for lo in range(0, s_ref.shape[1], chunk):
        part = pl.ds(lo, chunk)
        for i, (src, dst) in enumerate([(s_ref, s_hbm), (f_ref, f_hbm)]):
            copies.append(
                pltpu.make_async_copy(src.at[:, part], dst.at[:, part], sem.at[i, lo // chunk])
            )
    for c in copies:
        c.start()
    for c in copies:
        c.wait()


def on_device(initial, diffusivity, velocity, growth_rate, block_planes):
    shape = initial.shape
    plane = shape[1:]
    nodes = M // lax.axis_size("node")
    chunk = 2
    operands = [
        pltpu.with_memory_space_constraint(x, pltpu.HBM)
        for x in (block_planes, initial, diffusivity, velocity, growth_rate)
    ]
    vmem = pl.BlockSpec(memory_space=pltpu.VMEM)
    hbm = pl.BlockSpec(memory_space=pltpu.HBM)
    whole = jax.ShapeDtypeStruct((nodes,) + shape, jnp.float32)
    held = pl.pallas_call(
        functools.partial(window_kernel, moments()),
        out_shape=(whole, whole),
        in_specs=[hbm] * 5,
        out_specs=(vmem, vmem),
        scratch_shapes=[pltpu.SMEM(block_planes.shape, jnp.int32)]
        + [pltpu.VMEM(shape, jnp.float32)] * 5
        + [
            pltpu.VMEM((2, FAR) + plane, jnp.float32),
            pltpu.VMEM((2, FAR + 1) + plane, jnp.float32),
            pltpu.VMEM((5, nodes) + plane, jnp.float32),
            pltpu.SemaphoreType.DMA((8,)),
            pltpu.SemaphoreType.DMA((2, len(TRIPS))),
            pltpu.SemaphoreType.DMA((2, len(TRIPS))),
        ],
        compiler_params=pltpu.CompilerParams(
            collective_id=0, has_side_effects=True, vmem_limit_bytes=24 << 20
        ),
        name="window",
    )(*operands)
    return pl.pallas_call(
        functools.partial(write_kernel, chunk),
        out_shape=(whole, whole),
        in_specs=[vmem] * 2,
        out_specs=(hbm, hbm),
        scratch_shapes=[pltpu.SemaphoreType.DMA((2, shape[0] // chunk))],
        compiler_params=pltpu.CompilerParams(vmem_limit_bytes=24 << 20),
        name="write",
    )(*held)


def solution(mesh):
    placed = (
        P(("sample", "space"), None, None),
        P(("sample", "space"), None, None),
        P(("sample", "space"), None, None),
        P(("sample", "space"), None, None),
        P(),
    )
    return jax.shard_map(
        on_device,
        mesh=mesh,
        in_specs=placed,
        out_specs=(
            P("node", ("sample", "space"), None, None),
            P("node", ("sample", "space"), None, None),
        ),
        check_vma=False,
    )
```

```python
import functools
import math

import jax
import jax.numpy as jnp
from jax import lax
from jax.experimental import pallas as pl
from jax.experimental.pallas import tpu as pltpu
from jax.sharding import PartitionSpec as P

M = 8
step_length = 0.1

U, C, R, Y, FAR = 0, 1, 3, 4, 5
TRIPS = ((U, U, 1), (C, C, 2), (R, FAR, 1), (R, R, 1), (Y, Y, 1))


def legendre_values(order, position):
    previous_value = 1.0
    current_value = position
    for degree in range(2, order + 1):
        previous_value, current_value = (
            current_value,
            ((2 * degree - 1) * position * current_value - (degree - 1) * previous_value) / degree,
        )
    derivative = order * (position * current_value - previous_value) / (position * position - 1.0)
    return (current_value, derivative)


def collocation(count):
    descending = []
    for root_index in range(count):
        position = math.cos(math.pi * (root_index + 0.75) / (count + 0.5))
        for newton_step in range(60):
            poly_value, poly_slope = legendre_values(count, position)
            position = position - poly_value / poly_slope
        descending.append((position + 1.0) / 2.0)
    node_times = descending[::-1]
    quad_rows = []
    for row_index in range(count):
        quad_row = []
        for basis_index in range(count):
            coefficients = [1.0]
            for other_index in range(count):
                if other_index != basis_index:
                    denominator = node_times[basis_index] - node_times[other_index]
                    expanded = [0.0] * (len(coefficients) + 1)
                    for exponent, coefficient in enumerate(coefficients):
                        expanded[exponent + 1] += coefficient / denominator
                        expanded[exponent] -= coefficient * node_times[other_index] / denominator
                    coefficients = expanded
            integral = 0.0
            for exponent, coefficient in enumerate(coefficients):
                integral += coefficient * node_times[row_index] ** (exponent + 1) / (exponent + 1)
            quad_row.append(integral)
        quad_rows.append(quad_row)
    return (node_times, quad_rows)


def moments():
    _, quad = collocation(M)
    scale = [step_length * sum(row) for row in quad]
    rows = []
    for row in quad:
        power = [
            step_length * sum(q * s**k for q, s in zip(row, scale)) for k in range(4)
        ]
        rows.append((power[0], power[1], -3.0 * power[2], -power[3]))
    return rows


def across(u):
    rows, lanes = u.shape
    tile = [u[i : i + 8] for i in range(0, rows, 8)]
    row = lax.broadcasted_iota(jnp.int32, (8, lanes), 0)
    nil = jnp.zeros((8, lanes), u.dtype)
    down = [nil] + [pltpu.roll(t, 1, 0) for t in tile]
    rise = [pltpu.roll(t, 7, 0) for t in tile] + [nil]
    along_x = jnp.concatenate(
        [
            jnp.where(row == 0, down[k], down[k + 1]) + jnp.where(row == 7, rise[k + 1], rise[k])
            for k in range(len(tile))
        ],
        axis=0,
    )
    half = [u[:, i : i + 128] for i in range(0, lanes, 128)]
    lane = lax.broadcasted_iota(jnp.int32, (rows, 128), 1)
    nil = jnp.zeros((rows, 128), u.dtype)
    down = [nil] + [pltpu.roll(t, 1, 1) for t in half]
    rise = [pltpu.roll(t, 127, 1) for t in half] + [nil]
    along_y = jnp.concatenate(
        [
            jnp.where(lane == 0, down[k], down[k + 1])
            + jnp.where(lane == 127, rise[k + 1], rise[k])
            for k in range(len(half))
        ],
        axis=1,
    )
    return along_x + along_y


def factors(d_ref, v_ref, g_ref, p):
    d = d_ref[p]
    v = 0.5 * v_ref[p]
    return d, d - v, d + v, g_ref[p] - 6.0 * d


def window_kernel(
    table,
    bp_hbm, u_hbm, d_hbm, v_hbm, g_hbm, s_ref, f_ref,
    bp, u_ref, d_ref, v_ref, g_ref, r_ref, out, got, edge, load_sem, send_sem, recv_sem,
):
    me = lax.axis_index("space")
    count = lax.axis_size("space")
    cap = u_ref.shape[0]
    nodes = s_ref.shape[0]
    quarter = cap // 4
    pairs = [(bp_hbm, bp)]
    for i in range(4):
        part = pl.ds(i * quarter, cap - 3 * quarter if i == 3 else quarter)
        pairs.append((u_hbm.at[part], u_ref.at[part]))
    pairs += [(d_hbm, d_ref), (v_hbm, v_ref), (g_hbm, g_ref)]
    loads = [
        pltpu.make_async_copy(src, dst, load_sem.at[i]) for i, (src, dst) in enumerate(pairs)
    ]
    for load in loads:
        load.start()
    barrier = pltpu.get_barrier_semaphore()

    def exists(step):
        return jnp.logical_and(me + step >= 0, me + step < count)

    peers = 0
    for step in (-1, 1, -2, 2):

        @pl.when(exists(step))
        def _(step=step):
            pl.semaphore_signal(
                barrier, inc=1, device_id={"space": me + step}, device_id_type=pl.DeviceIdType.MESH
            )

        peers = peers + exists(step).astype(jnp.int32)
    nil = jnp.zeros(u_ref.shape[1:], jnp.float32)
    for side, step in ((0, -1), (1, 1)):

        @pl.when(jnp.logical_not(exists(step)))
        def _(side=side):
            for k in range(FAR):
                got[side, k] = nil

        @pl.when(jnp.logical_not(exists(2 * step)))
        def _(side=side):
            got[side, FAR] = nil

    node = lax.axis_index("node")
    weights = []
    for m in range(nodes):
        picked = [jnp.float32(x) for x in table[m]]
        for n in range(1, M // nodes):
            picked = [
                jnp.where(node == n, jnp.float32(x), y)
                for x, y in zip(table[n * nodes + m], picked)
            ]
        weights.append(picked)

    def copy(side, k):
        source, target, size = TRIPS[k]
        distance = 2 if target == FAR else 1
        step = distance if side == 0 else -distance
        return step, pltpu.make_async_remote_copy(
            src_ref=out.at[side, pl.ds(source, size)],
            dst_ref=got.at[side, pl.ds(target, size)],
            send_sem=send_sem.at[side, k],
            recv_sem=recv_sem.at[side, k],
            device_id={"space": me + step},
            device_id_type=pl.DeviceIdType.MESH,
        )

    def send(k):
        for side in range(2):
            step, c = copy(side, k)

            @pl.when(exists(step))
            def _(c=c):
                c.start()

    def receive(k):
        for side in range(2):
            step, c = copy(side, k)

            @pl.when(exists(-step))
            def _(c=c):
                c.wait_recv()

    loads[0].wait()
    length = bp[me]
    last = jnp.clip(length - 1, 0, cap - 1)
    single = last == 0

    def inner(ref, p):
        low = jnp.where(p == 0, 0.0, ref[jnp.maximum(p - 1, 0)])
        high = jnp.where(p == last, 0.0, ref[jnp.minimum(p + 1, cap - 1)])
        return low, high

    def first_rhs(p):
        d, rise, fall, own = factors(d_ref, v_ref, g_ref, p)
        low, high = inner(u_ref, p)
        u = u_ref[p]
        return d * across(u) + rise * high + fall * low + (own - u * u) * u

    def slope(p, r, low, high):
        d, rise, fall, own = factors(d_ref, v_ref, g_ref, p)
        u = u_ref[p]
        return d * across(r) + rise * high + fall * low + (own - 3.0 * (u * u)) * r

    def states_of(u, r, a):
        rr = r * r
        ur = u * rr
        cube = rr * r
        return [u + w[0] * r + w[1] * a + (w[2] * ur + w[3] * cube) for w in weights]

    for load in loads[1:5]:
        load.wait()
    out[0, U] = u_ref[last]
    out[1, U] = u_ref[0]
    pl.semaphore_wait(barrier, peers)
    send(0)
    for load in loads[5:]:
        load.wait()
    _, rise_l, fall_l, _ = factors(d_ref, v_ref, g_ref, last)
    _, rise_f, fall_f, _ = factors(d_ref, v_ref, g_ref, 0)
    out[0, C] = rise_l
    out[0, C + 1] = jnp.where(single, fall_l, 0.0)
    out[1, C] = fall_f
    out[1, C + 1] = jnp.where(single, rise_f, 0.0)
    send(1)

    def fill_r(p, carry):
        r_ref[p] = first_rhs(p)
        return carry

    lax.fori_loop(0, cap, fill_r, 0)
    receive(0)
    _, rise_l, fall_l, _ = factors(d_ref, v_ref, g_ref, last)
    _, rise_f, fall_f, _ = factors(d_ref, v_ref, g_ref, 0)
    r_l = r_ref[last] + rise_l * got[1, U] + jnp.where(single, fall_l * got[0, U], 0.0)
    r_f = r_ref[0] + fall_f * got[0, U] + jnp.where(single, rise_f * got[1, U], 0.0)
    out[0, R] = r_l
    out[1, R] = r_f
    send(2)
    send(3)
    r_ref[0] = r_f

    out[0, Y] = slope(last, out[0, R], *inner(r_ref, last))
    low, high = inner(r_ref, 0)
    out[1, Y] = slope(0, r_ref[0], low, jnp.where(last == 1, out[0, R], high))
    send(4)

    def fix_r(p, carry):
        r_ref[p] = jnp.where(p == last, out[0, R], r_ref[p])
        return carry

    lax.fori_loop(0, cap, fix_r, 0)

    def fill_s(p, carry):
        r = r_ref[p]
        values = states_of(u_ref[p], r, slope(p, r, *inner(r_ref, p)))
        live = p < length
        for m in range(nodes):
            s_ref[m, p] = jnp.where(live, values[m], 0.0)
        return carry

    lax.fori_loop(0, cap, fill_s, 0)

    def final(p, m, low, high):
        d, rise, fall, own = factors(d_ref, v_ref, g_ref, p)
        s = s_ref[m, p]
        f = d * across(s) + rise * high + fall * low + (own - s * s) * s
        return jnp.where(p < length, f, 0.0)

    def fill_f(p, carry):
        for m in range(nodes):
            low = s_ref[m, jnp.maximum(p - 1, 0)]
            high = s_ref[m, jnp.minimum(p + 1, cap - 1)]
            f_ref[m, p] = final(p, m, low, high)
        return carry

    lax.fori_loop(1, cap - 1, fill_f, 0)
    receive(3)
    values = states_of(
        u_ref[last],
        r_ref[last],
        out[0, Y] + rise_l * got[1, R] + jnp.where(single, fall_l * got[0, R], 0.0),
    )
    for m in range(nodes):
        edge[0, m] = values[m]
    values = states_of(
        u_ref[0],
        r_ref[0],
        out[1, Y] + fall_f * got[0, R] + jnp.where(single, rise_f * got[1, R], 0.0),
    )
    for m in range(nodes):
        s_ref[m, 0] = values[m]

    def fix_s(p, carry):
        for m in range(nodes):
            s_ref[m, p] = jnp.where(p == last, edge[0, m], s_ref[m, p])
        return carry

    lax.fori_loop(0, cap, fix_s, 0)
    receive(1)
    receive(2)
    receive(4)
    for side, r in ((0, r_ref[0]), (1, r_ref[last])):
        a = got[side, Y] + got[side, C] * r + got[side, C + 1] * got[side, FAR]
        values = states_of(got[side, U], got[side, R], a)
        for m in range(nodes):
            edge[1 + side, m] = values[m]

    def rim(p, m):
        low = jnp.where(p == 0, edge[1, m], s_ref[m, jnp.maximum(p - 1, 0)])
        high = jnp.where(p == last, edge[2, m], s_ref[m, jnp.minimum(p + 1, cap - 1)])
        return final(p, m, low, high)

    near = jnp.maximum(last - 1, 0)
    for m in range(nodes):
        f_ref[m, 0] = rim(0, m)
        f_ref[m, 1] = rim(1, m)
        edge[3, m] = rim(near, m)
        edge[4, m] = rim(last, m)

    def fix_f(p, carry):
        for m in range(nodes):
            f = jnp.where(p == near, edge[3, m], f_ref[m, p])
            f_ref[m, p] = jnp.where(p == last, edge[4, m], f)
        return carry

    lax.fori_loop(0, cap - 1, fix_f, 0)
    for m in range(nodes):
        f_ref[m, cap - 1] = jnp.where(last == cap - 1, edge[4, m], 0.0)
    for k in range(len(TRIPS)):
        for side in range(2):
            step, c = copy(side, k)

            @pl.when(exists(step))
            def _(c=c):
                c.wait_send()


def write_kernel(chunk, s_ref, f_ref, s_hbm, f_hbm, sem):
    copies = []
    for lo in range(0, s_ref.shape[1], chunk):
        part = pl.ds(lo, chunk)
        for i, (src, dst) in enumerate([(s_ref, s_hbm), (f_ref, f_hbm)]):
            copies.append(
                pltpu.make_async_copy(src.at[:, part], dst.at[:, part], sem.at[i, lo // chunk])
            )
    for c in copies:
        c.start()
    for c in copies:
        c.wait()


def on_device(initial, diffusivity, velocity, growth_rate, block_planes):
    shape = initial.shape
    plane = shape[1:]
    nodes = M // lax.axis_size("node")
    chunk = 4
    operands = [
        pltpu.with_memory_space_constraint(x, pltpu.HBM)
        for x in (block_planes, initial, diffusivity, velocity, growth_rate)
    ]
    vmem = pl.BlockSpec(memory_space=pltpu.VMEM)
    hbm = pl.BlockSpec(memory_space=pltpu.HBM)
    whole = jax.ShapeDtypeStruct((nodes,) + shape, jnp.float32)
    held = pl.pallas_call(
        functools.partial(window_kernel, moments()),
        out_shape=(whole, whole),
        in_specs=[hbm] * 5,
        out_specs=(vmem, vmem),
        scratch_shapes=[pltpu.SMEM(block_planes.shape, jnp.int32)]
        + [pltpu.VMEM(shape, jnp.float32)] * 5
        + [
            pltpu.VMEM((2, FAR) + plane, jnp.float32),
            pltpu.VMEM((2, FAR + 1) + plane, jnp.float32),
            pltpu.VMEM((5, nodes) + plane, jnp.float32),
            pltpu.SemaphoreType.DMA((8,)),
            pltpu.SemaphoreType.DMA((2, len(TRIPS))),
            pltpu.SemaphoreType.DMA((2, len(TRIPS))),
        ],
        compiler_params=pltpu.CompilerParams(
            collective_id=0, has_side_effects=True, vmem_limit_bytes=24 << 20
        ),
        name="window",
    )(*operands)
    return pl.pallas_call(
        functools.partial(write_kernel, chunk),
        out_shape=(whole, whole),
        in_specs=[vmem] * 2,
        out_specs=(hbm, hbm),
        scratch_shapes=[pltpu.SemaphoreType.DMA((2, shape[0] // chunk))],
        compiler_params=pltpu.CompilerParams(vmem_limit_bytes=24 << 20),
        name="write",
    )(*held)


def solution(mesh):
    placed = (
        P(("sample", "space"), None, None),
        P(("sample", "space"), None, None),
        P(("sample", "space"), None, None),
        P(("sample", "space"), None, None),
        P(),
    )
    return jax.shard_map(
        on_device,
        mesh=mesh,
        in_specs=placed,
        out_specs=(
            P("node", ("sample", "space"), None, None),
            P("node", ("sample", "space"), None, None),
        ),
        check_vma=False,
    )
```
